32 devices in a mesh: groups: 2 (over y), segment: 8 (over z, x), space: 2 (over core).
Axes of the slice: x: 2, y: 2, z: 4, core: 2. Of those that a mesh axis runs over, the one named last changes fastest.
Arguments:
- patches: bfloat16 [16, 256, 1536], P(('groups', 'segment'), 'space'), parts along dimension 0, may hold values from -120 to 120
- positions: int32 [16], P(('groups', 'segment')), parts along dimension 0, may hold values from 0 to 1
- timesteps: int32 [16], P(('groups', 'segment')), parts along dimension 0, may hold values from 0 to 1
- section_bounds: int32 [9], replicated, may hold values from 0 to 12, as said below
- tile_neighbours: int32 [4, 2], replicated, may hold values from 0 to 3, as said below
- modulation: bfloat16 [6, 12, 3, 1536], P('groups'), parts along dimension 0, may hold values from -9 to 9
- query_gain: float32 [12, 128], replicated, may hold values from 0.5 to 2
- stale_kv: bfloat16 [16, 2, 2, 512, 1536], P(('groups', 'segment'), None, None, 'space'), parts along dimension 0, may hold values from -70 to 70
Outputs:
- advanced: bfloat16 [16, 256, 1536], P(('groups', 'segment'), 'space'), parts along dimension 0
The draws below stay inside these ranges and needn't reach their ends.
There are 2 independent parts, one for each index of `groups`. The reference program is written for one: setup_inputs(seed, part) draws one part's arguments, and reference() takes and returns one part's arrays. A program takes and returns all parts, laid end to end along the dimension named above; an argument that names none is the same for every part. Nothing has to cross between parts.
Inputs may be any that keep to these rules, and one draw needn't show every extreme that they name: section_bounds[0] is 0 and section_bounds[8] is 12; section j holds layers section_bounds[j] to section_bounds[j+1] - 1, one or 2 of them, and some sections hold 2. `tile_neighbours`: tile g lies in time layer g // 2; row g names first a tile of its own time layer, then a tile of the other time layer.
All inputs are finite; a program needn't handle non-finite values.
Results may differ from the reference program's by a relative error of at most 0.0051.
Values may be sent and summed in bfloat16 or wider, within the bound.
A program may use at most 64 MiB of HBM per device.

```python
import math
import jax
import jax.numpy as jnp
from jax import lax

HEADS = 12
HDIM = 128
D = 1536
TILE = 128
GH = 2
GW = 1
SLAB_DEV = 2
NT = 4
NB = 2
PIPE = 8
LMAX = 2
LAYERS = 12
STEPS = 3
TICKS = 2
LANES = 1
PTOK = 256
PATCHES = 8
N_SEGMENT = 8
N_SPACE = 2


def draw_patches(key, part):
    drawn = jnp.clip(jax.random.normal(jax.random.fold_in(key, 31), (PATCHES, PTOK, D), jnp.float32), -4.0, 4.0)
    return drawn.astype(jnp.bfloat16)


def draw_section_bounds(key, part):
    shuffled = jax.random.permutation(jax.random.fold_in(key, 41), PIPE)
    counts = 1 + (shuffled < LAYERS - PIPE).astype(jnp.int32)
    bounds = jnp.concatenate([jnp.zeros((1,), jnp.int32), jnp.cumsum(counts).astype(jnp.int32)])
    return bounds


def draw_tile_neighbours(key, part):
    tile_ids = jnp.arange(NT, dtype=jnp.int32)
    layer_of = tile_ids // SLAB_DEV
    own_tile = layer_of * SLAB_DEV + jax.random.randint(jax.random.fold_in(key, 51), (NT,), 0, SLAB_DEV)
    other_tile = (1 - layer_of) * SLAB_DEV + jax.random.randint(jax.random.fold_in(key, 52), (NT,), 0, SLAB_DEV)
    return jnp.stack([own_tile, other_tile], axis=1).astype(jnp.int32)


def draw_modulation(key, part):
    shape_rows = (STEPS, LAYERS, D)
    shift_rows = 0.5 * jnp.clip(jax.random.normal(jax.random.fold_in(key, 21), shape_rows, jnp.float32), -4.0, 4.0)
    scale_rows = 0.3 * jnp.clip(jax.random.normal(jax.random.fold_in(key, 22), shape_rows, jnp.float32), -4.0, 4.0)
    gate_rows = 0.8 * jnp.clip(jax.random.normal(jax.random.fold_in(key, 23), shape_rows, jnp.float32), -4.0, 4.0)
    return jnp.stack([shift_rows, scale_rows, gate_rows], axis=2).astype(jnp.bfloat16)


def draw_stale_kv(key, part):
    key_part = jax.random.fold_in(key, 11)
    value_part = jax.random.fold_in(key, 12)
    shape_tiles = (N_SEGMENT, LMAX, NT, TILE, D)
    key_rows = jnp.clip(jax.random.normal(key_part, shape_tiles, jnp.float32), -4.0, 4.0)
    value_rows = 2.0 * jnp.clip(jax.random.normal(value_part, shape_tiles, jnp.float32), -4.0, 4.0)
    stacked = jnp.stack([key_rows, value_rows], axis=2)
    return stacked.reshape(N_SEGMENT, LMAX, 2, NT * TILE, D).astype(jnp.bfloat16)


def set_ends(entries, rng, least, top_value):
    dims = entries.shape
    spot = [jax.random.randint(jax.random.fold_in(rng, axis), (), 0, dims[axis]) for axis in range(len(dims))]
    entries = entries.at[tuple(spot)].set(least)
    longest = dims.index(max(dims))
    spot[longest] = (spot[longest] + 1) % dims[longest]
    return entries.at[tuple(spot)].set(top_value)


def setup_inputs(seed: int = 0, part: int = 0) -> dict:
    key_list = jax.random.split(jax.random.key(seed), 9)
    part_splits = jax.random.split(jax.random.fold_in(key_list[8], part), 9)
    return {
        "patches": draw_patches(jax.random.fold_in(jax.random.fold_in(key_list[8], part), 71), part),
        "positions": set_ends(jax.random.randint(part_splits[1], (PATCHES,), 0, GH * GW), jax.random.fold_in(part_splits[1], 1), 0, (GH * GW) - 1).astype(jnp.int32),
        "timesteps": set_ends(jax.random.randint(part_splits[2], (PATCHES,), 0, STEPS - 1), jax.random.fold_in(part_splits[2], 1), 0, (STEPS - 1) - 1).astype(jnp.int32),
        "section_bounds": draw_section_bounds(jax.random.fold_in(key_list[8], 71), part),
        "tile_neighbours": draw_tile_neighbours(jax.random.fold_in(key_list[8], 71), part),
        "modulation": draw_modulation(jax.random.fold_in(jax.random.fold_in(key_list[8], part), 71), part),
        "query_gain": jnp.clip(jnp.exp(jax.random.uniform(key_list[6], (LAYERS, HDIM), jnp.float32, math.log(0.5), math.log(2.0))), 0.5, 2.0),
        "stale_kv": draw_stale_kv(jax.random.fold_in(jax.random.fold_in(key_list[8], part), 71), part),
    }


epsilon = 1e-06

def attend(stream, key_tiles, value_tiles, tile_choice, mod_rows, gain_row):
    batch_size = stream.shape[0]
    middle = lax.optimization_barrier(jnp.mean(stream, axis=-1, keepdims=True))
    centred = stream - middle
    spread = lax.optimization_barrier(jnp.mean(centred * centred, axis=-1, keepdims=True))
    normed = centred * lax.rsqrt(spread + epsilon)
    shifted = normed * (1.0 + mod_rows[:, 1:2, :]) + mod_rows[:, 0:1, :]
    heads_in = shifted.reshape(batch_size, TILE, HEADS, HDIM)
    head_rms = lax.optimization_barrier(jnp.mean(heads_in * heads_in, axis=-1, keepdims=True))
    queries = (heads_in * lax.rsqrt(head_rms + epsilon) * gain_row).astype(jnp.bfloat16)
    key_rows = key_tiles[tile_choice].reshape(batch_size, NB * TILE, HEADS, HDIM)
    value_rows = value_tiles[tile_choice].reshape(batch_size, NB * TILE, HEADS, HDIM)
    scores = jnp.einsum('bqhd,bkhd->bhqk', queries.astype(jnp.float32), key_rows.astype(jnp.float32)) * HDIM ** (-0.5)
    row_max = lax.optimization_barrier(jnp.max(scores, axis=-1, keepdims=True))
    powers = jnp.exp(scores - row_max)
    totals = lax.optimization_barrier(jnp.sum(powers, axis=-1))
    weights = powers.astype(jnp.bfloat16)
    blended = jnp.einsum('bhqk,bkhd->bqhd', weights.astype(jnp.float32), value_rows.astype(jnp.float32))
    blended = blended / jnp.transpose(totals, (0, 2, 1))[..., None]
    return stream + mod_rows[:, 2:3, :] * blended.reshape(batch_size, TILE, D)

def run_section(stream, kv_slab, section, pos_one, step_one, section_bounds, tile_neighbours, modulation, query_gain):
    first_layer = section_bounds[section]
    layer_count = section_bounds[section + 1] - first_layer
    tile_states = stream.astype(jnp.float32).reshape(LANES * N_SPACE, TILE, D)
    core_ids = jnp.tile(jnp.arange(N_SPACE, dtype=jnp.int32), LANES)
    item_pos = jnp.repeat(pos_one, N_SPACE)
    item_step = jnp.repeat(step_one, N_SPACE)
    query_tile = core_ids * SLAB_DEV + item_pos
    tile_choice = tile_neighbours[query_tile]
    for slot_index in range(LMAX):
        layer_now = jnp.minimum(first_layer + slot_index, LAYERS - 1)
        mod_rows = modulation[item_step, layer_now].astype(jnp.float32)
        gain_row = query_gain[layer_now]
        key_tiles = kv_slab[slot_index, 0].reshape(NT, TILE, D)
        value_tiles = kv_slab[slot_index, 1].reshape(NT, TILE, D)
        updated = attend(tile_states, key_tiles, value_tiles, tile_choice, mod_rows, gain_row)
        tile_states = jnp.where(slot_index < layer_count, updated, tile_states)
    return tile_states.reshape(LANES, PTOK, D).astype(jnp.bfloat16)

def reference(patches, positions, timesteps, section_bounds, tile_neighbours, modulation, query_gain, stale_kv):
    holding = patches.reshape(N_SEGMENT, LANES, PTOK, D)
    pos_table = positions.reshape(N_SEGMENT, LANES)
    step_table = timesteps.reshape(N_SEGMENT, LANES)
    devices = jnp.arange(N_SEGMENT, dtype=jnp.int32)
    sections = devices % PIPE
    for tick_index in range(TICKS):
        root = (devices - tick_index) % N_SEGMENT
        crossed = (root % PIPE + tick_index >= PIPE).astype(jnp.int32)
        step_rows = step_table[root] + crossed[:, None]
        pos_rows = pos_table[root]

        def one_device(packed):
            stream, kv_slab, section, pos_one, step_one = packed
            return run_section(stream, kv_slab, section, pos_one, step_one, section_bounds, tile_neighbours, modulation, query_gain)
        updated = lax.map(one_device, (holding, stale_kv, sections, pos_rows, step_rows))
        holding = jnp.roll(updated, 1, axis=0)
    return holding.reshape(PATCHES, PTOK, D)
```

```python
import functools

import jax
import jax.numpy as jnp
from jax import lax
from jax.experimental import pallas as pl
from jax.experimental.pallas import tpu as pltpu
from jax.sharding import PartitionSpec as P

TICKS = 2
CHUNKS = 2
epsilon = 1e-06
MESH = pl.DeviceIdType.MESH


def window_kernel(
    cycle,
    pos_ref,
    step_ref,
    bounds_ref,
    near_ref,
    mod_ref,
    gain_ref,
    patch_ref,
    kv_ref,
    out_ref,
    own,
    staged,
    other,
    hold,
    fin,
    state,
    queries,
    meta_out,
    meta_in,
    meta_smem,
    table,
    own_sem,
    patch_sem,
    meta_send,
    meta_recv,
    meta_local,
    kv_send,
    kv_recv,
    state_send,
    state_recv,
):
    slots, _, slab_tiles, tile, width = kv_ref.shape
    chunks, rows = hold.shape[1], hold.shape[2]
    head_dim = gain_ref.shape[1]
    heads = width // head_dim
    pipe = bounds_ref.shape[0] - 1
    steps, layers = mod_ref.shape[0], mod_ref.shape[1]
    segment = lax.axis_index("segment")
    space = lax.axis_index("space")
    onward = lax.rem(segment + 1, cycle)
    behind = lax.rem(segment + cycle - 1, cycle)
    mate = 1 - space

    def own_copy(slot, part):
        return pltpu.make_async_copy(kv_ref.at[slot, part], own[slot][part], own_sem.at[slot, part])

    def kv_copy(tick, slot, part):
        return pltpu.make_async_remote_copy(
            src_ref=staged.at[tick, slot, part],
            dst_ref=other.at[tick, slot, part],
            send_sem=kv_send.at[tick, slot, part],
            recv_sem=kv_recv.at[tick, slot, part],
            device_id={"space": mate},
            device_id_type=MESH,
        )

    def state_copy(tick, chunk, target):
        return pltpu.make_async_remote_copy(
            src_ref=fin.at[tick, chunk],
            dst_ref=target,
            send_sem=state_send.at[tick, chunk],
            recv_sem=state_recv.at[tick, chunk],
            device_id={"segment": onward},
            device_id_type=MESH,
        )

    patch_copy = pltpu.make_async_copy(patch_ref, hold.at[0], patch_sem)
    meta_copy = pltpu.make_async_remote_copy(
        src_ref=meta_out,
        dst_ref=meta_in,
        send_sem=meta_send,
        recv_sem=meta_recv,
        device_id={"segment": onward},
        device_id_type=MESH,
    )
    order = [(slot, part) for slot in range(slots) for part in range(2)]
    for slot, part in order:
        own_copy(slot, part).start()
    patch_copy.start()

    barrier = pltpu.get_barrier_semaphore()
    pl.semaphore_signal(barrier, inc=1, device_id={"segment": onward}, device_id_type=MESH)
    pl.semaphore_signal(barrier, inc=1, device_id={"segment": behind}, device_id_type=MESH)
    pl.semaphore_signal(barrier, inc=1, device_id={"space": mate}, device_id_type=MESH)

    position = pos_ref[0]
    timestep = step_ref[0]
    table[0, 0] = position
    table[0, 1] = timestep
    lane = lax.broadcasted_iota(jnp.int32, meta_out.shape, 1)
    meta_out[...] = jnp.where(lane == 0, position, timestep)
    pl.semaphore_wait(barrier, 3)
    meta_copy.start()

    def wanted_by_mate(pos):
        return lax.rem(near_ref[mate * slab_tiles + pos, 1], slab_tiles)

    mate_tile = wanted_by_mate(position)
    for slot, part in order:
        own_copy(slot, part).wait()
        staged[0, slot, part] = own[slot][part][mate_tile]
        kv_copy(0, slot, part).start()
    patch_copy.wait()

    section = lax.rem(segment, pipe)
    first_layer = bounds_ref[section]
    layer_count = bounds_ref[section + 1] - first_layer
    to_exp2 = head_dim ** (-0.5) * 1.4426950408889634
    ones = jnp.ones((2 * tile, head_dim), jnp.bfloat16)

    def run(index, carry):
        tick = index // chunks
        chunk = lax.rem(index, chunks)

        @pl.when(index == 1)
        def _():
            meta_copy.wait_recv()
            to_smem = pltpu.make_async_copy(meta_in, meta_smem, meta_local)
            to_smem.start()
            to_smem.wait()
            table[1, 0] = meta_smem[0, 0]
            table[1, 1] = meta_smem[0, 1]
            later_tile = wanted_by_mate(meta_smem[0, 0])
            for slot, part in order:
                staged[1, slot, part] = own[slot][part][later_tile]
                kv_copy(1, slot, part).start()

        @pl.when(tick == 1)
        def _():
            state_copy(0, chunk, hold.at[1, chunk]).wait_recv()

        root = lax.rem(segment - tick + cycle, cycle)
        crossed = jnp.where(lax.rem(root, pipe) + tick >= pipe, 1, 0)
        step_row = jnp.minimum(table[tick, 1] + crossed, steps - 1)
        own_tile = lax.rem(near_ref[space * slab_tiles + table[tick, 0], 0], slab_tiles)
        state[...] = hold[tick, chunk].astype(jnp.float32)

        for slot in range(slots):
            layer = jnp.minimum(first_layer + slot, layers - 1)
            mod = mod_ref[step_row, layer].astype(jnp.float32)
            gain = gain_ref[pl.ds(layer, 1), :]
            active = jnp.where(slot < layer_count, 1.0, 0.0)
            gate = mod[2:3] * active
            spans = [pl.ds(head * head_dim, head_dim) for head in range(heads)]
            total = state[:, spans[0]]
            for span in spans[1:]:
                total = total + state[:, span]
            middle = jnp.sum(total, axis=-1, keepdims=True) * (1.0 / width)
            total = jnp.zeros((rows, head_dim), jnp.float32)
            for span in spans:
                centred = state[:, span] - middle
                total = total + centred * centred
            spread = jnp.sum(total, axis=-1, keepdims=True) * (1.0 / width)
            scale = lax.rsqrt(spread + epsilon)
            for head, span in enumerate(spans):
                cols = slice(head * head_dim, (head + 1) * head_dim)
                normed = (state[:, span] - middle) * scale
                shifted = normed * (1.0 + mod[1:2, cols]) + mod[0:1, cols]
                rms = jnp.sum(shifted * shifted, axis=-1, keepdims=True) * (1.0 / head_dim)
                queries[:, span] = (shifted * lax.rsqrt(rms + epsilon) * gain).astype(jnp.bfloat16)

            @pl.when(chunk == 0)
            def _():
                for part in range(2):
                    kv_copy(tick, slot, part).wait_recv()

            for head, span in enumerate(spans):
                cols = slice(head * head_dim, (head + 1) * head_dim)
                keys = jnp.concatenate(
                    [own[slot][0][own_tile, :, span], other[tick, slot, 0, :, span]], axis=0
                )
                values = jnp.concatenate(
                    [own[slot][1][own_tile, :, span], other[tick, slot, 1, :, span]], axis=0
                )
                scores = lax.dot_general(
                    queries[:, span], keys, (((1,), (1,)), ((), ())), preferred_element_type=jnp.float32
                )
                top = jnp.max(scores, axis=-1, keepdims=True)
                weights = jnp.exp2((scores - top) * to_exp2).astype(jnp.bfloat16)
                blended = lax.dot_general(
                    weights,
                    jnp.concatenate([values, ones], axis=1),
                    (((1,), (0,)), ((), ())),
                    preferred_element_type=jnp.float32,
                )
                state[:, span] += gate[:, cols] * (blended[:, :head_dim] / blended[:, head_dim:])

        fin[tick, chunk] = state[...].astype(jnp.bfloat16)

        @pl.when(tick == 0)
        def _():
            state_copy(0, chunk, hold.at[1, chunk]).start()

        @pl.when(tick == 1)
        def _():
            state_copy(1, chunk, out_ref.at[chunk]).start()

        return carry

    lax.fori_loop(0, TICKS * chunks, run, 0)

    meta_copy.wait_send()
    for tick in range(TICKS):
        for slot, part in order:
            kv_copy(tick, slot, part).wait_send()
    for chunk in range(chunks):
        state_copy(0, chunk, hold.at[1, chunk]).wait_send()
        state_copy(1, chunk, out_ref.at[chunk]).wait()


def per_device(
    patches, positions, timesteps, section_bounds, tile_neighbours, modulation, query_gain, stale_kv
):
    _, tile, width = patches.shape
    _, slots, _, slab_rows, _ = stale_kv.shape
    slab_tiles = slab_rows // tile
    rows = tile // CHUNKS
    cycle = lax.axis_size("segment")
    kv = stale_kv.reshape(slots, 2, slab_tiles, tile, width)
    smem = pl.BlockSpec(memory_space=pltpu.SMEM)
    vmem = pl.BlockSpec(memory_space=pltpu.VMEM)
    anywhere = pl.BlockSpec(memory_space=pl.ANY)
    dma = pltpu.SemaphoreType.DMA
    flops = TICKS * slots * 4 * tile * 2 * tile * width
    advanced = pl.pallas_call(
        functools.partial(window_kernel, cycle),
        out_shape=jax.ShapeDtypeStruct((CHUNKS, rows, width), patches.dtype),
        in_specs=[smem, smem, smem, smem, vmem, vmem, anywhere, anywhere],
        out_specs=anywhere,
        scratch_shapes=[
            [[pltpu.VMEM(kv.shape[2:], kv.dtype) for _ in range(2)] for _ in range(slots)],
            pltpu.VMEM((TICKS, slots, 2, tile, width), kv.dtype),
            pltpu.VMEM((TICKS, slots, 2, tile, width), kv.dtype),
            pltpu.VMEM((TICKS, CHUNKS, rows, width), jnp.bfloat16),
            pltpu.VMEM((TICKS, CHUNKS, rows, width), jnp.bfloat16),
            pltpu.VMEM((rows, width), jnp.float32),
            pltpu.VMEM((rows, width), jnp.bfloat16),
            pltpu.VMEM((8, 128), jnp.int32),
            pltpu.VMEM((8, 128), jnp.int32),
            pltpu.SMEM((8, 128), jnp.int32),
            pltpu.SMEM((TICKS, 2), jnp.int32),
            dma((slots, 2)),
            dma,
            dma,
            dma,
            dma,
            dma((TICKS, slots, 2)),
            dma((TICKS, slots, 2)),
            dma((TICKS, CHUNKS)),
            dma((TICKS, CHUNKS)),
        ],
        compiler_params=pltpu.CompilerParams(
            collective_id=0, has_side_effects=True, vmem_limit_bytes=58 * 2**20
        ),
        cost_estimate=pl.CostEstimate(
            flops=flops, bytes_accessed=kv.size * 2 + patches.size * 4, transcendentals=0
        ),
    )(
        positions,
        timesteps,
        section_bounds,
        tile_neighbours,
        modulation,
        query_gain,
        patches.reshape(CHUNKS, rows, width),
        kv,
    )
    return advanced.reshape(patches.shape)


def solution(mesh):
    placed = (
        P(("groups", "segment"), "space", None),
        P(("groups", "segment")),
        P(("groups", "segment")),
        P(),
        P(),
        P("groups", None, None, None),
        P(),
        P(("groups", "segment"), None, None, "space", None),
    )
    return jax.shard_map(
        per_device,
        mesh=mesh,
        in_specs=placed,
        out_specs=P(("groups", "segment"), "space", None),
        check_vma=False,
    )
```

```python
import functools

import jax
import jax.numpy as jnp
from jax import lax
from jax.experimental import pallas as pl
from jax.experimental.pallas import tpu as pltpu
from jax.sharding import PartitionSpec as P

TICKS = 2
CHUNKS = 2
epsilon = 1e-06
MESH = pl.DeviceIdType.MESH


def window_kernel(
    cycle,
    pos_ref,
    step_ref,
    bounds_ref,
    near_ref,
    mod_ref,
    gain_ref,
    patch_ref,
    kv_ref,
    out_ref,
    own,
    staged,
    other,
    hold,
    fin,
    state,
    queries,
    meta_out,
    meta_in,
    meta_smem,
    table,
    own_sem,
    patch_sem,
    meta_send,
    meta_recv,
    meta_local,
    kv_send,
    kv_recv,
    state_send,
    state_recv,
):
    slots, _, slab_tiles, tile, width = kv_ref.shape
    chunks, rows = hold.shape[1], hold.shape[2]
    head_dim = gain_ref.shape[1]
    heads = width // head_dim
    pipe = bounds_ref.shape[0] - 1
    steps, layers = mod_ref.shape[0], mod_ref.shape[1]
    segment = lax.axis_index("segment")
    space = lax.axis_index("space")
    onward = lax.rem(segment + 1, cycle)
    behind = lax.rem(segment + cycle - 1, cycle)
    mate = 1 - space

    def own_copy(slot, part):
        return pltpu.make_async_copy(kv_ref.at[slot, part], own[slot][part], own_sem.at[slot, part])

    def kv_copy(tick, slot, part):
        return pltpu.make_async_remote_copy(
            src_ref=staged.at[tick, slot, part],
            dst_ref=other.at[tick, slot, part],
            send_sem=kv_send.at[tick, slot, part],
            recv_sem=kv_recv.at[tick, slot, part],
            device_id={"space": mate},
            device_id_type=MESH,
        )

    def state_copy(tick, chunk, target):
        return pltpu.make_async_remote_copy(
            src_ref=fin.at[tick, chunk],
            dst_ref=target,
            send_sem=state_send.at[tick, chunk],
            recv_sem=state_recv.at[tick, chunk],
            device_id={"segment": onward},
            device_id_type=MESH,
        )

    patch_copy = pltpu.make_async_copy(patch_ref, hold.at[0], patch_sem)
    meta_copy = pltpu.make_async_remote_copy(
        src_ref=meta_out,
        dst_ref=meta_in,
        send_sem=meta_send,
        recv_sem=meta_recv,
        device_id={"segment": onward},
        device_id_type=MESH,
    )
    order = [(slot, part) for slot in range(slots) for part in range(2)]
    for slot, part in order:
        own_copy(slot, part).start()
    patch_copy.start()

    barrier = pltpu.get_barrier_semaphore()
    pl.semaphore_signal(barrier, inc=1, device_id={"segment": behind}, device_id_type=MESH)
    pl.semaphore_signal(barrier, inc=1, device_id={"space": mate}, device_id_type=MESH)

    position = pos_ref[0]
    timestep = step_ref[0]
    table[0, 0] = position
    table[0, 1] = timestep
    lane = lax.broadcasted_iota(jnp.int32, meta_out.shape, 1)
    meta_out[...] = jnp.where(lane == 0, position, timestep)
    pl.semaphore_wait(barrier, 2)
    meta_copy.start()

    def wanted_by_mate(pos):
        return lax.rem(near_ref[1, mate * slab_tiles + pos], slab_tiles)

    mate_tile = wanted_by_mate(position)
    for slot, part in order:
        own_copy(slot, part).wait()
        staged[0, slot, part] = own[slot][part][mate_tile]
        kv_copy(0, slot, part).start()
    patch_copy.wait()

    section = lax.rem(segment, pipe)
    first_layer = bounds_ref[section]
    layer_count = bounds_ref[section + 1] - first_layer
    to_exp2 = head_dim ** (-0.5) * 1.4426950408889634
    ones = jnp.ones((2 * tile, head_dim), jnp.bfloat16)

    def run(index, carry):
        tick = index // chunks
        chunk = lax.rem(index, chunks)

        @pl.when(index == 1)
        def _():
            meta_copy.wait_recv()
            to_smem = pltpu.make_async_copy(meta_in, meta_smem, meta_local)
            to_smem.start()
            to_smem.wait()
            table[1, 0] = meta_smem[0, 0]
            table[1, 1] = meta_smem[0, 1]
            later_tile = wanted_by_mate(meta_smem[0, 0])
            for slot, part in order:
                staged[1, slot, part] = own[slot][part][later_tile]
                kv_copy(1, slot, part).start()

        @pl.when(tick == 1)
        def _():
            state_copy(0, chunk, hold.at[1, chunk]).wait_recv()

        root = lax.rem(segment - tick + cycle, cycle)
        crossed = jnp.where(lax.rem(root, pipe) + tick >= pipe, 1, 0)
        step_row = jnp.minimum(table[tick, 1] + crossed, steps - 1)
        own_tile = lax.rem(near_ref[0, space * slab_tiles + table[tick, 0]], slab_tiles)
        state[...] = hold[tick, chunk].astype(jnp.float32)

        for slot in range(slots):
            layer = jnp.minimum(first_layer + slot, layers - 1)
            mod = mod_ref[step_row, layer].astype(jnp.float32)
            gain = gain_ref[pl.ds(layer, 1), :]
            active = jnp.where(slot < layer_count, 1.0, 0.0)
            gate = mod[2:3] * active
            spans = [pl.ds(head * head_dim, head_dim) for head in range(heads)]
            total = state[:, spans[0]]
            for span in spans[1:]:
                total = total + state[:, span]
            middle = jnp.sum(total, axis=-1, keepdims=True) * (1.0 / width)
            total = jnp.zeros((rows, head_dim), jnp.float32)
            for span in spans:
                centred = state[:, span] - middle
                total = total + centred * centred
            spread = jnp.sum(total, axis=-1, keepdims=True) * (1.0 / width)
            scale = lax.rsqrt(spread + epsilon)
            for head, span in enumerate(spans):
                cols = slice(head * head_dim, (head + 1) * head_dim)
                normed = (state[:, span] - middle) * scale
                shifted = normed * (1.0 + mod[1:2, cols]) + mod[0:1, cols]
                rms = jnp.sum(shifted * shifted, axis=-1, keepdims=True) * (1.0 / head_dim)
                queries[:, span] = (shifted * lax.rsqrt(rms + epsilon) * gain).astype(jnp.bfloat16)

            @pl.when(chunk == 0)
            def _():
                for part in range(2):
                    kv_copy(tick, slot, part).wait_recv()

            for head, span in enumerate(spans):
                cols = slice(head * head_dim, (head + 1) * head_dim)
                keys = jnp.concatenate(
                    [own[slot][0][own_tile, :, span], other[tick, slot, 0, :, span]], axis=0
                )
                values = jnp.concatenate(
                    [own[slot][1][own_tile, :, span], other[tick, slot, 1, :, span]], axis=0
                )
                scores = lax.dot_general(
                    queries[:, span], keys, (((1,), (1,)), ((), ())), preferred_element_type=jnp.float32
                )
                top = jnp.max(scores, axis=-1, keepdims=True)
                weights = jnp.exp2((scores - top) * to_exp2).astype(jnp.bfloat16)
                blended = lax.dot_general(
                    weights,
                    jnp.concatenate([values, ones], axis=1),
                    (((1,), (0,)), ((), ())),
                    preferred_element_type=jnp.float32,
                )
                state[:, span] += gate[:, cols] * (blended[:, :head_dim] / blended[:, head_dim:])

        fin[tick, chunk] = state[...].astype(jnp.bfloat16)

        @pl.when(tick == 0)
        def _():
            state_copy(0, chunk, hold.at[1, chunk]).start()

        @pl.when(tick == 1)
        def _():
            state_copy(1, chunk, out_ref.at[chunk]).start()

        return carry

    lax.fori_loop(0, TICKS * chunks, run, 0)

    meta_copy.wait_send()
    for tick in range(TICKS):
        for slot, part in order:
            kv_copy(tick, slot, part).wait_send()
    for chunk in range(chunks):
        state_copy(0, chunk, hold.at[1, chunk]).wait_send()
        state_copy(1, chunk, out_ref.at[chunk]).wait()


def per_device(
    patches, positions, timesteps, section_bounds, tile_neighbours, modulation, query_gain, stale_kv
):
    _, tile, width = patches.shape
    _, slots, _, slab_rows, _ = stale_kv.shape
    slab_tiles = slab_rows // tile
    rows = tile // CHUNKS
    cycle = lax.axis_size("segment")
    kv = stale_kv.reshape(slots, 2, slab_tiles, tile, width)
    smem = pl.BlockSpec(memory_space=pltpu.SMEM)
    vmem = pl.BlockSpec(memory_space=pltpu.VMEM)
    anywhere = pl.BlockSpec(memory_space=pl.ANY)
    dma = pltpu.SemaphoreType.DMA
    flops = TICKS * slots * 4 * tile * 2 * tile * width
    advanced = pl.pallas_call(
        functools.partial(window_kernel, cycle),
        out_shape=jax.ShapeDtypeStruct((CHUNKS, rows, width), patches.dtype),
        in_specs=[smem, smem, smem, smem, vmem, vmem, anywhere, anywhere],
        out_specs=anywhere,
        scratch_shapes=[
            [[pltpu.VMEM(kv.shape[2:], kv.dtype) for _ in range(2)] for _ in range(slots)],
            pltpu.VMEM((TICKS, slots, 2, tile, width), kv.dtype),
            pltpu.VMEM((TICKS, slots, 2, tile, width), kv.dtype),
            pltpu.VMEM((TICKS, CHUNKS, rows, width), jnp.bfloat16),
            pltpu.VMEM((TICKS, CHUNKS, rows, width), jnp.bfloat16),
            pltpu.VMEM((rows, width), jnp.float32),
            pltpu.VMEM((rows, width), jnp.bfloat16),
            pltpu.VMEM((8, 128), jnp.int32),
            pltpu.VMEM((8, 128), jnp.int32),
            pltpu.SMEM((8, 128), jnp.int32),
            pltpu.SMEM((TICKS, 2), jnp.int32),
            dma((slots, 2)),
            dma,
            dma,
            dma,
            dma,
            dma((TICKS, slots, 2)),
            dma((TICKS, slots, 2)),
            dma((TICKS, CHUNKS)),
            dma((TICKS, CHUNKS)),
        ],
        compiler_params=pltpu.CompilerParams(
            collective_id=0, has_side_effects=True, vmem_limit_bytes=52 * 2**20
        ),
        cost_estimate=pl.CostEstimate(
            flops=flops, bytes_accessed=kv.size * 2 + patches.size * 4, transcendentals=0
        ),
    )(
        positions,
        timesteps,
        section_bounds,
        tile_neighbours.T,
        modulation,
        query_gain,
        patches.reshape(CHUNKS, rows, width),
        kv,
    )
    return advanced.reshape(patches.shape)


def solution(mesh):
    placed = (
        P(("groups", "segment"), "space", None),
        P(("groups", "segment")),
        P(("groups", "segment")),
        P(),
        P(),
        P("groups", None, None, None),
        P(),
        P(("groups", "segment"), None, None, "space", None),
    )
    return jax.shard_map(
        per_device,
        mesh=mesh,
        in_specs=placed,
        out_specs=P(("groups", "segment"), "space", None),
        check_vma=False,
    )
```

```python
import functools

import jax
import jax.numpy as jnp
from jax import lax
from jax.experimental import pallas as pl
from jax.experimental.pallas import tpu as pltpu
from jax.sharding import PartitionSpec as P

TICKS = 2
CHUNKS = 4
epsilon = 1e-06
MESH = pl.DeviceIdType.MESH


def window_kernel(
    cycle,
    pos_ref,
    step_ref,
    bounds_ref,
    near_ref,
    mod_hbm,
    gain_hbm,
    patch_ref,
    kv_ref,
    out_ref,
    mod_ref,
    gain_ref,
    own,
    staged,
    other,
    hold,
    fin,
    state,
    queries,
    meta_out,
    meta_in,
    meta_smem,
    table,
    own_sem,
    mod_sem,
    gain_sem,
    patch_sem,
    meta_send,
    meta_recv,
    meta_local,
    kv_send,
    kv_recv,
    state_send,
    state_recv,
):
    slots, _, slab_tiles, tile, width = kv_ref.shape
    chunks, rows = hold.shape[1], hold.shape[2]
    head_dim = gain_ref.shape[1]
    heads = width // head_dim
    pipe = bounds_ref.shape[0] - 1
    steps, layers = mod_ref.shape[0], mod_ref.shape[1]
    segment = lax.axis_index("segment")
    space = lax.axis_index("space")
    onward = lax.rem(segment + 1, cycle)
    behind = lax.rem(segment + cycle - 1, cycle)
    mate = 1 - space

    def own_copy(slot, part):
        return pltpu.make_async_copy(kv_ref.at[slot, part], own[slot][part], own_sem.at[slot, part])

    def kv_copy(tick, slot, part):
        return pltpu.make_async_remote_copy(
            src_ref=staged.at[tick, slot, part],
            dst_ref=other.at[tick, slot, part],
            send_sem=kv_send.at[tick, slot, part],
            recv_sem=kv_recv.at[tick, slot, part],
            device_id={"space": mate},
            device_id_type=MESH,
        )

    def state_copy(tick, chunk, target):
        return pltpu.make_async_remote_copy(
            src_ref=fin.at[tick, chunk],
            dst_ref=target,
            send_sem=state_send.at[tick, chunk],
            recv_sem=state_recv.at[tick, chunk],
            device_id={"segment": onward},
            device_id_type=MESH,
        )

    patch_copy = pltpu.make_async_copy(patch_ref, hold.at[0], patch_sem)
    mod_copy = pltpu.make_async_copy(mod_hbm, mod_ref, mod_sem)
    gain_copy = pltpu.make_async_copy(gain_hbm, gain_ref, gain_sem)
    meta_copy = pltpu.make_async_remote_copy(
        src_ref=meta_out,
        dst_ref=meta_in,
        send_sem=meta_send,
        recv_sem=meta_recv,
        device_id={"segment": onward},
        device_id_type=MESH,
    )
    order = [(slot, part) for slot in range(slots) for part in range(2)]
    for slot, part in order:
        own_copy(slot, part).start()
    patch_copy.start()
    mod_copy.start()
    gain_copy.start()

    barrier = pltpu.get_barrier_semaphore()
    pl.semaphore_signal(barrier, inc=1, device_id={"segment": behind}, device_id_type=MESH)
    pl.semaphore_signal(barrier, inc=1, device_id={"space": mate}, device_id_type=MESH)

    position = pos_ref[0]
    timestep = step_ref[0]
    table[0, 0] = position
    table[0, 1] = timestep
    lane = lax.broadcasted_iota(jnp.int32, meta_out.shape, 1)
    meta_out[...] = jnp.where(lane == 0, position, timestep)
    pl.semaphore_wait(barrier, 2)
    meta_copy.start()

    def wanted_by_mate(pos):
        return lax.rem(near_ref[1, mate * slab_tiles + pos], slab_tiles)

    mate_tile = wanted_by_mate(position)
    for slot, part in order:
        own_copy(slot, part).wait()
        staged[0, slot, part] = own[slot][part][mate_tile]
        kv_copy(0, slot, part).start()
    patch_copy.wait()
    mod_copy.wait()
    gain_copy.wait()

    section = lax.rem(segment, pipe)
    first_layer = bounds_ref[section]
    layer_count = bounds_ref[section + 1] - first_layer
    to_exp2 = head_dim ** (-0.5) * 1.4426950408889634
    ones = jnp.ones((2 * tile, head_dim), jnp.bfloat16)

    def run(index, carry):
        tick = index // chunks
        chunk = lax.rem(index, chunks)

        @pl.when(index == 1)
        def _():
            meta_copy.wait_recv()
            to_smem = pltpu.make_async_copy(meta_in, meta_smem, meta_local)
            to_smem.start()
            to_smem.wait()
            table[1, 0] = meta_smem[0, 0]
            table[1, 1] = meta_smem[0, 1]
            later_tile = wanted_by_mate(meta_smem[0, 0])
            for slot, part in order:
                staged[1, slot, part] = own[slot][part][later_tile]
                kv_copy(1, slot, part).start()

        @pl.when(tick == 1)
        def _():
            state_copy(0, chunk, hold.at[1, chunk]).wait_recv()

        root = lax.rem(segment - tick + cycle, cycle)
        crossed = jnp.where(lax.rem(root, pipe) + tick >= pipe, 1, 0)
        step_row = jnp.minimum(table[tick, 1] + crossed, steps - 1)
        own_tile = lax.rem(near_ref[0, space * slab_tiles + table[tick, 0]], slab_tiles)
        state[...] = hold[tick, chunk].astype(jnp.float32)

        for slot in range(slots):
            layer = jnp.minimum(first_layer + slot, layers - 1)
            mod = mod_ref[step_row, layer].astype(jnp.float32)
            gain = gain_ref[pl.ds(layer, 1), :]
            active = jnp.where(slot < layer_count, 1.0, 0.0)
            gate = mod[2:3] * active
            spans = [pl.ds(head * head_dim, head_dim) for head in range(heads)]
            total = state[:, spans[0]]
            for span in spans[1:]:
                total = total + state[:, span]
            middle = jnp.sum(total, axis=-1, keepdims=True) * (1.0 / width)
            total = jnp.zeros((rows, head_dim), jnp.float32)
            for span in spans:
                centred = state[:, span] - middle
                total = total + centred * centred
            spread = jnp.sum(total, axis=-1, keepdims=True) * (1.0 / width)
            scale = lax.rsqrt(spread + epsilon)
            for head, span in enumerate(spans):
                cols = slice(head * head_dim, (head + 1) * head_dim)
                normed = (state[:, span] - middle) * scale
                shifted = normed * (1.0 + mod[1:2, cols]) + mod[0:1, cols]
                rms = jnp.sum(shifted * shifted, axis=-1, keepdims=True) * (1.0 / head_dim)
                queries[:, span] = (shifted * lax.rsqrt(rms + epsilon) * gain).astype(jnp.bfloat16)

            @pl.when(chunk == 0)
            def _():
                for part in range(2):
                    kv_copy(tick, slot, part).wait_recv()

            for head, span in enumerate(spans):
                cols = slice(head * head_dim, (head + 1) * head_dim)
                keys = jnp.concatenate(
                    [own[slot][0][own_tile, :, span], other[tick, slot, 0, :, span]], axis=0
                )
                values = jnp.concatenate(
                    [own[slot][1][own_tile, :, span], other[tick, slot, 1, :, span]], axis=0
                )
                scores = lax.dot_general(
                    queries[:, span], keys, (((1,), (1,)), ((), ())), preferred_element_type=jnp.float32
                )
                top = jnp.max(scores, axis=-1, keepdims=True)
                weights = jnp.exp2((scores - top) * to_exp2).astype(jnp.bfloat16)
                blended = lax.dot_general(
                    weights,
                    jnp.concatenate([values, ones], axis=1),
                    (((1,), (0,)), ((), ())),
                    preferred_element_type=jnp.float32,
                )
                state[:, span] += gate[:, cols] * (blended[:, :head_dim] / blended[:, head_dim:])

        fin[tick, chunk] = state[...].astype(jnp.bfloat16)

        @pl.when(tick == 0)
        def _():
            state_copy(0, chunk, hold.at[1, chunk]).start()

        @pl.when(tick == 1)
        def _():
            state_copy(1, chunk, out_ref.at[chunk]).start()

        return carry

    lax.fori_loop(0, TICKS * chunks, run, 0)

    meta_copy.wait_send()
    for tick in range(TICKS):
        for slot, part in order:
            kv_copy(tick, slot, part).wait_send()
    for chunk in range(chunks):
        state_copy(0, chunk, hold.at[1, chunk]).wait_send()
        state_copy(1, chunk, out_ref.at[chunk]).wait()


def per_device(
    patches, positions, timesteps, section_bounds, tile_neighbours, modulation, query_gain, stale_kv
):
    _, tile, width = patches.shape
    _, slots, _, slab_rows, _ = stale_kv.shape
    slab_tiles = slab_rows // tile
    rows = tile // CHUNKS
    cycle = lax.axis_size("segment")
    kv = stale_kv.reshape(slots, 2, slab_tiles, tile, width)
    smem = pl.BlockSpec(memory_space=pltpu.SMEM)
    hbm = pl.BlockSpec(memory_space=pltpu.HBM)
    anywhere = pl.BlockSpec(memory_space=pl.ANY)
    dma = pltpu.SemaphoreType.DMA
    flops = TICKS * slots * 4 * tile * 2 * tile * width
    advanced = pl.pallas_call(
        functools.partial(window_kernel, cycle),
        out_shape=pltpu.VMEM((CHUNKS, rows, width), patches.dtype),
        in_specs=[smem, smem, smem, smem, hbm, hbm, hbm, hbm],
        out_specs=anywhere,
        scratch_shapes=[
            pltpu.VMEM(modulation.shape, modulation.dtype),
            pltpu.VMEM(query_gain.shape, query_gain.dtype),
            [[pltpu.VMEM(kv.shape[2:], kv.dtype) for _ in range(2)] for _ in range(slots)],
            pltpu.VMEM((TICKS, slots, 2, tile, width), kv.dtype),
            pltpu.VMEM((TICKS, slots, 2, tile, width), kv.dtype),
            pltpu.VMEM((TICKS, CHUNKS, rows, width), jnp.bfloat16),
            pltpu.VMEM((TICKS, CHUNKS, rows, width), jnp.bfloat16),
            pltpu.VMEM((rows, width), jnp.float32),
            pltpu.VMEM((rows, width), jnp.bfloat16),
            pltpu.VMEM((8, 128), jnp.int32),
            pltpu.VMEM((8, 128), jnp.int32),
            pltpu.SMEM((8, 128), jnp.int32),
            pltpu.SMEM((TICKS, 2), jnp.int32),
            dma((slots, 2)),
            dma,
            dma,
            dma,
            dma,
            dma,
            dma,
            dma((TICKS, slots, 2)),
            dma((TICKS, slots, 2)),
            dma((TICKS, CHUNKS)),
            dma((TICKS, CHUNKS)),
        ],
        compiler_params=pltpu.CompilerParams(
            collective_id=0, has_side_effects=True, vmem_limit_bytes=58 * 2**20
        ),
        cost_estimate=pl.CostEstimate(
            flops=flops, bytes_accessed=kv.size * 2 + patches.size * 4, transcendentals=0
        ),
    )(
        positions,
        timesteps,
        section_bounds,
        tile_neighbours.T,
        modulation,
        query_gain,
        patches.reshape(CHUNKS, rows, width),
        kv,
    )
    return advanced.reshape(patches.shape)


def solution(mesh):
    placed = (
        P(("groups", "segment"), "space", None),
        P(("groups", "segment")),
        P(("groups", "segment")),
        P(),
        P(),
        P("groups", None, None, None),
        P(),
        P(("groups", "segment"), None, None, "space", None),
    )
    return jax.shard_map(
        per_device,
        mesh=mesh,
        in_specs=placed,
        out_specs=P(("groups", "segment"), "space", None),
        check_vma=False,
    )
```

```python
import functools

import jax
import jax.numpy as jnp
from jax import lax
from jax.experimental import pallas as pl
from jax.experimental.pallas import tpu as pltpu
from jax.sharding import PartitionSpec as P

TICKS = 2
CHUNKS = 2
AHEAD = 3
epsilon = 1e-06
MESH = pl.DeviceIdType.MESH


def window_kernel(
    cycle,
    pos_ref,
    step_ref,
    bounds_ref,
    near_ref,
    mod_hbm,
    gain_hbm,
    patch_ref,
    kv_ref,
    out_ref,
    mod_ref,
    gain_ref,
    own,
    staged,
    other,
    hold,
    fin,
    state,
    queries,
    meta_out,
    meta_in,
    meta_smem,
    table,
    own_sem,
    mod_sem,
    gain_sem,
    patch_sem,
    meta_send,
    meta_recv,
    meta_local,
    kv_send,
    kv_recv,
    state_send,
    state_recv,
):
    slots, _, slab_tiles, tile, width = kv_ref.shape
    chunks, rows = hold.shape[1], hold.shape[2]
    head_dim = gain_ref.shape[1]
    heads = width // head_dim
    pipe = bounds_ref.shape[0] - 1
    steps, layers = mod_ref.shape[0], mod_ref.shape[1]
    segment = lax.axis_index("segment")
    space = lax.axis_index("space")
    onward = lax.rem(segment + 1, cycle)
    behind = lax.rem(segment + cycle - 1, cycle)
    mate = 1 - space

    def own_copy(slot, part):
        return pltpu.make_async_copy(kv_ref.at[slot, part], own[slot][part], own_sem.at[slot, part])

    def kv_copy(tick, slot, part):
        return pltpu.make_async_remote_copy(
            src_ref=staged.at[tick, slot, part],
            dst_ref=other.at[tick, slot, part],
            send_sem=kv_send.at[tick, slot, part],
            recv_sem=kv_recv.at[tick, slot, part],
            device_id={"space": mate},
            device_id_type=MESH,
        )

    def state_copy(tick, chunk, target):
        return pltpu.make_async_remote_copy(
            src_ref=fin.at[tick, chunk],
            dst_ref=target,
            send_sem=state_send.at[tick, chunk],
            recv_sem=state_recv.at[tick, chunk],
            device_id={"segment": onward},
            device_id_type=MESH,
        )

    patch_copy = pltpu.make_async_copy(patch_ref, hold.at[0], patch_sem)
    mod_copy = pltpu.make_async_copy(mod_hbm, mod_ref, mod_sem)
    gain_copy = pltpu.make_async_copy(gain_hbm, gain_ref, gain_sem)
    meta_copy = pltpu.make_async_remote_copy(
        src_ref=meta_out,
        dst_ref=meta_in,
        send_sem=meta_send,
        recv_sem=meta_recv,
        device_id={"segment": onward},
        device_id_type=MESH,
    )
    order = [(slot, part) for slot in range(slots) for part in range(2)]
    for slot, part in order:
        own_copy(slot, part).start()
    patch_copy.start()
    mod_copy.start()
    gain_copy.start()

    barrier = pltpu.get_barrier_semaphore()
    pl.semaphore_signal(barrier, inc=1, device_id={"segment": behind}, device_id_type=MESH)
    pl.semaphore_signal(barrier, inc=1, device_id={"space": mate}, device_id_type=MESH)

    position = pos_ref[0]
    timestep = step_ref[0]
    table[0, 0] = position
    table[0, 1] = timestep
    lane = lax.broadcasted_iota(jnp.int32, meta_out.shape, 1)
    meta_out[...] = jnp.where(lane == 0, position, timestep)
    pl.semaphore_wait(barrier, 2)
    meta_copy.start()

    def wanted_by_mate(pos):
        return lax.rem(near_ref[1, mate * slab_tiles + pos], slab_tiles)

    mate_tile = wanted_by_mate(position)
    for slot, part in order:
        own_copy(slot, part).wait()
        staged[0, slot, part] = own[slot][part][mate_tile]
        kv_copy(0, slot, part).start()
    patch_copy.wait()
    mod_copy.wait()
    gain_copy.wait()

    section = lax.rem(segment, pipe)
    first_layer = bounds_ref[section]
    layer_count = bounds_ref[section + 1] - first_layer
    to_exp2 = head_dim ** (-0.5) * 1.4426950408889634

    def run(index, carry):
        tick = index // chunks
        chunk = lax.rem(index, chunks)

        @pl.when(index == 1)
        def _():
            meta_copy.wait_recv()
            to_smem = pltpu.make_async_copy(meta_in, meta_smem, meta_local)
            to_smem.start()
            to_smem.wait()
            table[1, 0] = meta_smem[0, 0]
            table[1, 1] = meta_smem[0, 1]
            later_tile = wanted_by_mate(meta_smem[0, 0])
            for slot, part in order:
                staged[1, slot, part] = own[slot][part][later_tile]
                kv_copy(1, slot, part).start()

        @pl.when(tick == 1)
        def _():
            state_copy(0, chunk, hold.at[1, chunk]).wait_recv()

        root = lax.rem(segment - tick + cycle, cycle)
        crossed = jnp.where(lax.rem(root, pipe) + tick >= pipe, 1, 0)
        step_row = jnp.minimum(table[tick, 1] + crossed, steps - 1)
        own_tile = lax.rem(near_ref[0, space * slab_tiles + table[tick, 0]], slab_tiles)
        state[...] = hold[tick, chunk].astype(jnp.float32)

        for slot in range(slots):
            layer = jnp.minimum(first_layer + slot, layers - 1)
            mod = mod_ref[step_row, layer].astype(jnp.float32)
            gain = gain_ref[pl.ds(layer, 1), :]
            active = jnp.where(slot < layer_count, 1.0, 0.0)
            gate = mod[2:3] * active
            spans = [pl.ds(head * head_dim, head_dim) for head in range(heads)]
            total = state[:, spans[0]]
            for span in spans[1:]:
                total = total + state[:, span]
            middle = jnp.sum(total, axis=-1, keepdims=True) * (1.0 / width)
            total = jnp.zeros((rows, head_dim), jnp.float32)
            for span in spans:
                centred = state[:, span] - middle
                total = total + centred * centred
            spread = jnp.sum(total, axis=-1, keepdims=True) * (1.0 / width)
            scale = lax.rsqrt(spread + epsilon)
            for head, span in enumerate(spans):
                cols = slice(head * head_dim, (head + 1) * head_dim)
                normed = (state[:, span] - middle) * scale
                shifted = normed * (1.0 + mod[1:2, cols]) + mod[0:1, cols]
                rms = jnp.sum(shifted * shifted, axis=-1, keepdims=True) * (1.0 / head_dim)
                queries[:, span] = (shifted * lax.rsqrt(rms + epsilon) * gain).astype(jnp.bfloat16)

            @pl.when(chunk == 0)
            def _():
                for part in range(2):
                    kv_copy(tick, slot, part).wait_recv()

            def score(head):
                keys = jnp.concatenate(
                    [own[slot][0][own_tile, :, spans[head]], other[tick, slot, 0, :, spans[head]]], axis=0
                )
                return lax.dot_general(
                    queries[:, spans[head]], keys, (((1,), (1,)), ((), ())), preferred_element_type=jnp.float32
                )

            def weigh(scores):
                top = jnp.max(scores, axis=-1, keepdims=True)
                powers = jnp.exp2((scores - top) * to_exp2)
                total = jnp.sum(powers, axis=-1, keepdims=True)
                guess = pl.reciprocal(total, approx=True)
                return powers.astype(jnp.bfloat16), guess * (2.0 - total * guess)

            def blend(head, weights):
                values = jnp.concatenate(
                    [own[slot][1][own_tile, :, spans[head]], other[tick, slot, 1, :, spans[head]]], axis=0
                )
                return lax.dot_general(
                    weights, values, (((1,), (0,)), ((), ())), preferred_element_type=jnp.float32
                )

            def settle(head, blended, inverse):
                cols = slice(head * head_dim, (head + 1) * head_dim)
                state[:, spans[head]] += gate[:, cols] * (blended * inverse)

            ahead = [score(head) for head in range(min(AHEAD, heads))]
            mixing = []
            for head in range(heads):
                if head + AHEAD < heads:
                    ahead.append(score(head + AHEAD))
                weights, inverse = weigh(ahead[head])
                mixing.append((blend(head, weights), inverse))
                if head >= 1:
                    settle(head - 1, *mixing[head - 1])
            settle(heads - 1, *mixing[heads - 1])

        fin[tick, chunk] = state[...].astype(jnp.bfloat16)

        @pl.when(tick == 0)
        def _():
            state_copy(0, chunk, hold.at[1, chunk]).start()

        @pl.when(tick == 1)
        def _():
            state_copy(1, chunk, out_ref.at[chunk]).start()

        return carry

    lax.fori_loop(0, TICKS * chunks, run, 0)

    meta_copy.wait_send()
    for tick in range(TICKS):
        for slot, part in order:
            kv_copy(tick, slot, part).wait_send()
    for chunk in range(chunks):
        state_copy(0, chunk, hold.at[1, chunk]).wait_send()
        state_copy(1, chunk, out_ref.at[chunk]).wait()


def per_device(
    patches, positions, timesteps, section_bounds, tile_neighbours, modulation, query_gain, stale_kv
):
    _, tile, width = patches.shape
    _, slots, _, slab_rows, _ = stale_kv.shape
    slab_tiles = slab_rows // tile
    rows = tile // CHUNKS
    cycle = lax.axis_size("segment")
    kv = stale_kv.reshape(slots, 2, slab_tiles, tile, width)
    smem = pl.BlockSpec(memory_space=pltpu.SMEM)
    hbm = pl.BlockSpec(memory_space=pltpu.HBM)
    anywhere = pl.BlockSpec(memory_space=pl.ANY)
    dma = pltpu.SemaphoreType.DMA
    flops = TICKS * slots * 4 * tile * 2 * tile * width
    advanced = pl.pallas_call(
        functools.partial(window_kernel, cycle),
        out_shape=pltpu.VMEM((CHUNKS, rows, width), patches.dtype),
        in_specs=[smem, smem, smem, smem, hbm, hbm, hbm, hbm],
        out_specs=anywhere,
        scratch_shapes=[
            pltpu.VMEM(modulation.shape, modulation.dtype),
            pltpu.VMEM(query_gain.shape, query_gain.dtype),
            [[pltpu.VMEM(kv.shape[2:], kv.dtype) for _ in range(2)] for _ in range(slots)],
            pltpu.VMEM((TICKS, slots, 2, tile, width), kv.dtype),
            pltpu.VMEM((TICKS, slots, 2, tile, width), kv.dtype),
            pltpu.VMEM((TICKS, CHUNKS, rows, width), jnp.bfloat16),
            pltpu.VMEM((TICKS, CHUNKS, rows, width), jnp.bfloat16),
            pltpu.VMEM((rows, width), jnp.float32),
            pltpu.VMEM((rows, width), jnp.bfloat16),
            pltpu.VMEM((8, 128), jnp.int32),
            pltpu.VMEM((8, 128), jnp.int32),
            pltpu.SMEM((8, 128), jnp.int32),
            pltpu.SMEM((TICKS, 2), jnp.int32),
            dma((slots, 2)),
            dma,
            dma,
            dma,
            dma,
            dma,
            dma,
            dma((TICKS, slots, 2)),
            dma((TICKS, slots, 2)),
            dma((TICKS, CHUNKS)),
            dma((TICKS, CHUNKS)),
        ],
        compiler_params=pltpu.CompilerParams(
            collective_id=0, has_side_effects=True, vmem_limit_bytes=58 * 2**20
        ),
        cost_estimate=pl.CostEstimate(
            flops=flops, bytes_accessed=kv.size * 2 + patches.size * 4, transcendentals=0
        ),
    )(
        positions,
        timesteps,
        section_bounds,
        tile_neighbours.T,
        modulation,
        query_gain,
        patches.reshape(CHUNKS, rows, width),
        kv,
    )
    return advanced.reshape(patches.shape)


def solution(mesh):
    placed = (
        P(("groups", "segment"), "space", None),
        P(("groups", "segment")),
        P(("groups", "segment")),
        P(),
        P(),
        P("groups", None, None, None),
        P(),
        P(("groups", "segment"), None, None, "space", None),
    )
    return jax.shard_map(
        per_device,
        mesh=mesh,
        in_specs=placed,
        out_specs=P(("groups", "segment"), "space", None),
        check_vma=False,
    )
```

```python
import functools

import jax
import jax.numpy as jnp
from jax import lax
from jax.experimental import pallas as pl
from jax.experimental.pallas import tpu as pltpu
from jax.sharding import PartitionSpec as P

TICKS = 2
CHUNKS = 2
AHEAD = 3
epsilon = 1e-06
MESH = pl.DeviceIdType.MESH


def window_kernel(
    cycle,
    pos_ref,
    step_ref,
    bounds_ref,
    near_ref,
    mod_hbm,
    gain_hbm,
    patch_ref,
    kv_ref,
    out_ref,
    mod_ref,
    gain_ref,
    own,
    staged,
    other,
    hold,
    fin,
    state,
    bent,
    squares,
    queries,
    meta_out,
    meta_in,
    meta_smem,
    table,
    own_sem,
    mod_sem,
    gain_sem,
    patch_sem,
    meta_send,
    meta_recv,
    meta_local,
    kv_send,
    kv_recv,
    state_send,
    state_recv,
):
    slots, _, slab_tiles, tile, width = kv_ref.shape
    chunks, rows = hold.shape[1], hold.shape[2]
    head_dim = gain_ref.shape[1]
    heads = width // head_dim
    pipe = bounds_ref.shape[0] - 1
    steps, layers = mod_ref.shape[0], mod_ref.shape[1]
    segment = lax.axis_index("segment")
    space = lax.axis_index("space")
    onward = lax.rem(segment + 1, cycle)
    behind = lax.rem(segment + cycle - 1, cycle)
    mate = 1 - space

    def own_copy(slot, part):
        return pltpu.make_async_copy(kv_ref.at[slot, part], own[slot][part], own_sem.at[slot, part])

    def kv_copy(tick, slot, part):
        return pltpu.make_async_remote_copy(
            src_ref=staged.at[tick, slot, part],
            dst_ref=other.at[tick, slot, part],
            send_sem=kv_send.at[tick, slot, part],
            recv_sem=kv_recv.at[tick, slot, part],
            device_id={"space": mate},
            device_id_type=MESH,
        )

    def state_copy(tick, chunk, target):
        return pltpu.make_async_remote_copy(
            src_ref=fin.at[tick, chunk],
            dst_ref=target,
            send_sem=state_send.at[tick, chunk],
            recv_sem=state_recv.at[tick, chunk],
            device_id={"segment": onward},
            device_id_type=MESH,
        )

    patch_copy = pltpu.make_async_copy(patch_ref, hold.at[0], patch_sem)
    mod_copy = pltpu.make_async_copy(mod_hbm, mod_ref, mod_sem)
    gain_copy = pltpu.make_async_copy(gain_hbm, gain_ref, gain_sem)
    meta_copy = pltpu.make_async_remote_copy(
        src_ref=meta_out,
        dst_ref=meta_in,
        send_sem=meta_send,
        recv_sem=meta_recv,
        device_id={"segment": onward},
        device_id_type=MESH,
    )
    order = [(slot, part) for slot in range(slots) for part in range(2)]
    for slot, part in order:
        own_copy(slot, part).start()
    patch_copy.start()
    mod_copy.start()
    gain_copy.start()

    barrier = pltpu.get_barrier_semaphore()
    pl.semaphore_signal(barrier, inc=1, device_id={"segment": behind}, device_id_type=MESH)
    pl.semaphore_signal(barrier, inc=1, device_id={"space": mate}, device_id_type=MESH)

    position = pos_ref[0]
    timestep = step_ref[0]
    table[0, 0] = position
    table[0, 1] = timestep
    lane = lax.broadcasted_iota(jnp.int32, meta_out.shape, 1)
    meta_out[...] = jnp.where(lane == 0, position, timestep)
    pl.semaphore_wait(barrier, 2)
    meta_copy.start()

    def wanted_by_mate(pos):
        return lax.rem(near_ref[1, mate * slab_tiles + pos], slab_tiles)

    mate_tile = wanted_by_mate(position)
    for slot, part in order:
        own_copy(slot, part).wait()
        staged[0, slot, part] = own[slot][part][mate_tile]
        kv_copy(0, slot, part).start()
    patch_copy.wait()
    mod_copy.wait()
    gain_copy.wait()

    section = lax.rem(segment, pipe)
    first_layer = bounds_ref[section]
    layer_count = bounds_ref[section + 1] - first_layer
    to_exp2 = head_dim ** (-0.5) * 1.4426950408889634

    ones = jnp.ones((2 * tile, head_dim), jnp.bfloat16)

    def run(index, carry):
        tick = index // chunks
        chunk = lax.rem(index, chunks)

        @pl.when(index == 1)
        def _():
            meta_copy.wait_recv()
            to_smem = pltpu.make_async_copy(meta_in, meta_smem, meta_local)
            to_smem.start()
            to_smem.wait()
            table[1, 0] = meta_smem[0, 0]
            table[1, 1] = meta_smem[0, 1]
            later_tile = wanted_by_mate(meta_smem[0, 0])
            for slot, part in order:
                staged[1, slot, part] = own[slot][part][later_tile]
                kv_copy(1, slot, part).start()

        @pl.when(tick == 1)
        def _():
            state_copy(0, chunk, hold.at[1, chunk]).wait_recv()

        root = lax.rem(segment - tick + cycle, cycle)
        crossed = jnp.where(lax.rem(root, pipe) + tick >= pipe, 1, 0)
        step_row = jnp.minimum(table[tick, 1] + crossed, steps - 1)
        own_tile = lax.rem(near_ref[0, space * slab_tiles + table[tick, 0]], slab_tiles)
        state[...] = hold[tick, chunk].astype(jnp.float32)

        for slot in range(slots):
            layer = jnp.minimum(first_layer + slot, layers - 1)
            mod = mod_ref[step_row, layer].astype(jnp.float32)
            gain = gain_ref[pl.ds(layer, 1), :]
            active = jnp.where(slot < layer_count, 1.0, 0.0)
            gate = mod[2:3] * active
            spans = [pl.ds(head * head_dim, head_dim) for head in range(heads)]
            total = state[:, spans[0]]
            for span in spans[1:]:
                total = total + state[:, span]
            middle = jnp.sum(total, axis=-1, keepdims=True) * (1.0 / width)
            total = jnp.zeros((rows, head_dim), jnp.float32)
            for span in spans:
                centred = state[:, span] - middle
                total = total + centred * centred
            spread = jnp.sum(total, axis=-1, keepdims=True) * (1.0 / width)
            scale = lax.rsqrt(spread + epsilon)
            for head, span in enumerate(spans):
                cols = slice(head * head_dim, (head + 1) * head_dim)
                normed = (state[:, span] - middle) * scale
                shifted = normed * (1.0 + mod[1:2, cols]) + mod[0:1, cols]
                bent[:, span] = shifted
                squares[pl.ds(head * rows, rows), :] = (shifted * shifted).astype(jnp.bfloat16)
            square_sums = jnp.dot(squares[...], ones[:head_dim], preferred_element_type=jnp.float32)
            for head, span in enumerate(spans):
                rms = square_sums[head * rows : (head + 1) * rows] * (1.0 / head_dim)
                queries[:, span] = (bent[:, span] * lax.rsqrt(rms + epsilon) * gain).astype(jnp.bfloat16)

            @pl.when(chunk == 0)
            def _():
                for part in range(2):
                    kv_copy(tick, slot, part).wait_recv()

            def score(head):
                keys = jnp.concatenate(
                    [own[slot][0][own_tile, :, spans[head]], other[tick, slot, 0, :, spans[head]]], axis=0
                )
                return lax.dot_general(
                    queries[:, spans[head]], keys, (((1,), (1,)), ((), ())), preferred_element_type=jnp.float32
                )

            def weigh(scores):
                top = jnp.max(scores, axis=-1, keepdims=True)
                return jnp.exp2((scores - top) * to_exp2).astype(jnp.bfloat16)

            def blend(head, weights):
                values = jnp.concatenate(
                    [own[slot][1][own_tile, :, spans[head]], other[tick, slot, 1, :, spans[head]]], axis=0
                )
                return lax.dot_general(
                    weights,
                    jnp.concatenate([values, ones], axis=1),
                    (((1,), (0,)), ((), ())),
                    preferred_element_type=jnp.float32,
                )

            def settle(head, mixed):
                cols = slice(head * head_dim, (head + 1) * head_dim)
                total = mixed[:, head_dim:]
                guess = pl.reciprocal(total, approx=True)
                inverse = guess * (2.0 - total * guess)
                state[:, spans[head]] += gate[:, cols] * (mixed[:, :head_dim] * inverse)

            ahead = [score(head) for head in range(min(AHEAD, heads))]
            mixing = []
            for head in range(heads):
                if head + AHEAD < heads:
                    ahead.append(score(head + AHEAD))
                mixing.append(blend(head, weigh(ahead[head])))
                if head >= 1:
                    settle(head - 1, mixing[head - 1])
            settle(heads - 1, mixing[heads - 1])

        fin[tick, chunk] = state[...].astype(jnp.bfloat16)

        @pl.when(tick == 0)
        def _():
            state_copy(0, chunk, hold.at[1, chunk]).start()

        @pl.when(tick == 1)
        def _():
            state_copy(1, chunk, out_ref.at[chunk]).start()

        return carry

    lax.fori_loop(0, TICKS * chunks, run, 0)

    meta_copy.wait_send()
    for tick in range(TICKS):
        for slot, part in order:
            kv_copy(tick, slot, part).wait_send()
    for chunk in range(chunks):
        state_copy(0, chunk, hold.at[1, chunk]).wait_send()
        state_copy(1, chunk, out_ref.at[chunk]).wait()


def per_device(
    patches, positions, timesteps, section_bounds, tile_neighbours, modulation, query_gain, stale_kv
):
    _, tile, width = patches.shape
    _, slots, _, slab_rows, _ = stale_kv.shape
    slab_tiles = slab_rows // tile
    rows = tile // CHUNKS
    cycle = lax.axis_size("segment")
    kv = stale_kv.reshape(slots, 2, slab_tiles, tile, width)
    smem = pl.BlockSpec(memory_space=pltpu.SMEM)
    hbm = pl.BlockSpec(memory_space=pltpu.HBM)
    anywhere = pl.BlockSpec(memory_space=pl.ANY)
    dma = pltpu.SemaphoreType.DMA
    flops = TICKS * slots * 4 * tile * 2 * tile * width
    advanced = pl.pallas_call(
        functools.partial(window_kernel, cycle),
        out_shape=pltpu.VMEM((CHUNKS, rows, width), patches.dtype),
        in_specs=[smem, smem, smem, smem, hbm, hbm, hbm, hbm],
        out_specs=anywhere,
        scratch_shapes=[
            pltpu.VMEM(modulation.shape, modulation.dtype),
            pltpu.VMEM(query_gain.shape, query_gain.dtype),
            [[pltpu.VMEM(kv.shape[2:], kv.dtype) for _ in range(2)] for _ in range(slots)],
            pltpu.VMEM((TICKS, slots, 2, tile, width), kv.dtype),
            pltpu.VMEM((TICKS, slots, 2, tile, width), kv.dtype),
            pltpu.VMEM((TICKS, CHUNKS, rows, width), jnp.bfloat16),
            pltpu.VMEM((TICKS, CHUNKS, rows, width), jnp.bfloat16),
            pltpu.VMEM((rows, width), jnp.float32),
            pltpu.VMEM((rows, width), jnp.float32),
            pltpu.VMEM((width // query_gain.shape[1] * rows, query_gain.shape[1]), jnp.bfloat16),
            pltpu.VMEM((rows, width), jnp.bfloat16),
            pltpu.VMEM((8, 128), jnp.int32),
            pltpu.VMEM((8, 128), jnp.int32),
            pltpu.SMEM((8, 128), jnp.int32),
            pltpu.SMEM((TICKS, 2), jnp.int32),
            dma((slots, 2)),
            dma,
            dma,
            dma,
            dma,
            dma,
            dma,
            dma((TICKS, slots, 2)),
            dma((TICKS, slots, 2)),
            dma((TICKS, CHUNKS)),
            dma((TICKS, CHUNKS)),
        ],
        compiler_params=pltpu.CompilerParams(
            collective_id=0, has_side_effects=True, vmem_limit_bytes=58 * 2**20
        ),
        cost_estimate=pl.CostEstimate(
            flops=flops, bytes_accessed=kv.size * 2 + patches.size * 4, transcendentals=0
        ),
    )(
        positions,
        timesteps,
        section_bounds,
        tile_neighbours.T,
        modulation,
        query_gain,
        patches.reshape(CHUNKS, rows, width),
        kv,
    )
    return advanced.reshape(patches.shape)


def solution(mesh):
    placed = (
        P(("groups", "segment"), "space", None),
        P(("groups", "segment")),
        P(("groups", "segment")),
        P(),
        P(),
        P("groups", None, None, None),
        P(),
        P(("groups", "segment"), None, None, "space", None),
    )
    return jax.shard_map(
        per_device,
        mesh=mesh,
        in_specs=placed,
        out_specs=P(("groups", "segment"), "space", None),
        check_vma=False,
    )
```

```python
import functools

import jax
import jax.numpy as jnp
from jax import lax
from jax.experimental import pallas as pl
from jax.experimental.pallas import tpu as pltpu
from jax.sharding import PartitionSpec as P

TICKS = 2
CHUNKS = 2
AHEAD = 3
epsilon = 1e-06
MESH = pl.DeviceIdType.MESH


def window_kernel(
    cycle,
    pos_ref,
    step_ref,
    bounds_ref,
    near_ref,
    mod_hbm,
    gain_hbm,
    patch_ref,
    kv_ref,
    out_ref,
    mod_ref,
    gain_ref,
    own,
    staged,
    other,
    hold,
    fin,
    state,
    bent,
    squares,
    queries,
    meta_out,
    meta_in,
    meta_smem,
    table,
    own_sem,
    mod_sem,
    gain_sem,
    patch_sem,
    meta_send,
    meta_recv,
    meta_local,
    kv_send,
    kv_recv,
    state_send,
    state_recv,
):
    slots, _, slab_tiles, tile, width = kv_ref.shape
    chunks, rows = hold.shape[1], hold.shape[2]
    head_dim = gain_ref.shape[1]
    heads = width // head_dim
    pipe = bounds_ref.shape[0] - 1
    steps, layers = mod_ref.shape[0], mod_ref.shape[1]
    segment = lax.axis_index("segment")
    space = lax.axis_index("space")
    onward = lax.rem(segment + 1, cycle)
    behind = lax.rem(segment + cycle - 1, cycle)
    mate = 1 - space

    def own_copy(slot, part):
        return pltpu.make_async_copy(kv_ref.at[slot, part], own[slot][part], own_sem.at[slot, part])

    def kv_copy(tick, slot, part):
        return pltpu.make_async_remote_copy(
            src_ref=staged.at[tick, slot, part],
            dst_ref=other.at[tick, slot, part],
            send_sem=kv_send.at[tick, slot, part],
            recv_sem=kv_recv.at[tick, slot, part],
            device_id={"space": mate},
            device_id_type=MESH,
        )

    def state_copy(tick, chunk, target):
        return pltpu.make_async_remote_copy(
            src_ref=fin.at[tick, chunk],
            dst_ref=target,
            send_sem=state_send.at[tick, chunk],
            recv_sem=state_recv.at[tick, chunk],
            device_id={"segment": onward},
            device_id_type=MESH,
        )

    patch_copy = pltpu.make_async_copy(patch_ref, hold.at[0], patch_sem)
    mod_copy = pltpu.make_async_copy(mod_hbm, mod_ref, mod_sem)
    gain_copy = pltpu.make_async_copy(gain_hbm, gain_ref, gain_sem)
    meta_copy = pltpu.make_async_remote_copy(
        src_ref=meta_out,
        dst_ref=meta_in,
        send_sem=meta_send,
        recv_sem=meta_recv,
        device_id={"segment": onward},
        device_id_type=MESH,
    )
    order = [(slot, part) for slot in range(slots) for part in range(2)]
    for slot, part in order:
        own_copy(slot, part).start()
    patch_copy.start()
    mod_copy.start()
    gain_copy.start()

    barrier = pltpu.get_barrier_semaphore()
    pl.semaphore_signal(barrier, inc=1, device_id={"segment": behind}, device_id_type=MESH)
    pl.semaphore_signal(barrier, inc=1, device_id={"space": mate}, device_id_type=MESH)

    position = pos_ref[0]
    timestep = step_ref[0]
    table[0, 0] = position
    table[0, 1] = timestep
    lane = lax.broadcasted_iota(jnp.int32, meta_out.shape, 1)
    meta_out[...] = jnp.where(lane == 0, position, timestep)
    pl.semaphore_wait(barrier, 2)
    meta_copy.start()

    def wanted_by_mate(pos):
        return lax.rem(near_ref[1, mate * slab_tiles + pos], slab_tiles)

    mate_tile = wanted_by_mate(position)
    for slot, part in order:
        own_copy(slot, part).wait()
        staged[0, slot, part] = own[slot][part][mate_tile]
        kv_copy(0, slot, part).start()
    patch_copy.wait()
    mod_copy.wait()
    gain_copy.wait()

    section = lax.rem(segment, pipe)
    first_layer = bounds_ref[section]
    layer_count = bounds_ref[section + 1] - first_layer
    to_exp2 = head_dim ** (-0.5) * 1.4426950408889634

    ones = jnp.ones((2 * tile, head_dim), jnp.bfloat16)

    def run(index, carry):
        tick = index // chunks
        chunk = lax.rem(index, chunks)

        @pl.when(tick == 1)
        def _():
            state_copy(0, chunk, hold.at[1, chunk]).wait_recv()

        root = lax.rem(segment - tick + cycle, cycle)
        crossed = jnp.where(lax.rem(root, pipe) + tick >= pipe, 1, 0)
        step_row = jnp.minimum(table[tick, 1] + crossed, steps - 1)
        own_tile = lax.rem(near_ref[0, space * slab_tiles + table[tick, 0]], slab_tiles)
        state[...] = hold[tick, chunk].astype(jnp.float32)

        for slot in range(slots):
            layer = jnp.minimum(first_layer + slot, layers - 1)
            mod = mod_ref[step_row, layer].astype(jnp.float32)
            gain = gain_ref[pl.ds(layer, 1), :]
            active = jnp.where(slot < layer_count, 1.0, 0.0)
            gate = mod[2:3] * active
            spans = [pl.ds(head * head_dim, head_dim) for head in range(heads)]
            total = state[:, spans[0]]
            for span in spans[1:]:
                total = total + state[:, span]
            middle = jnp.sum(total, axis=-1, keepdims=True) * (1.0 / width)
            total = jnp.zeros((rows, head_dim), jnp.float32)
            for span in spans:
                centred = state[:, span] - middle
                total = total + centred * centred
            spread = jnp.sum(total, axis=-1, keepdims=True) * (1.0 / width)
            scale = lax.rsqrt(spread + epsilon)
            for head, span in enumerate(spans):
                cols = slice(head * head_dim, (head + 1) * head_dim)
                normed = (state[:, span] - middle) * scale
                shifted = normed * (1.0 + mod[1:2, cols]) + mod[0:1, cols]
                bent[:, span] = shifted
                squares[pl.ds(head * rows, rows), :] = (shifted * shifted).astype(jnp.bfloat16)
            square_sums = jnp.dot(squares[...], ones[:head_dim], preferred_element_type=jnp.float32)
            for head, span in enumerate(spans):
                rms = square_sums[head * rows : (head + 1) * rows] * (1.0 / head_dim)
                queries[:, span] = (bent[:, span] * lax.rsqrt(rms + epsilon) * gain).astype(jnp.bfloat16)

            @pl.when(chunk == 0)
            def _():
                for part in range(2):
                    kv_copy(tick, slot, part).wait_recv()

            @pl.when(index == 0)
            def _():
                if slot == 0:
                    meta_copy.wait_recv()
                    to_smem = pltpu.make_async_copy(meta_in, meta_smem, meta_local)
                    to_smem.start()
                    to_smem.wait()
                    table[1, 0] = meta_smem[0, 0]
                    table[1, 1] = meta_smem[0, 1]
                later_tile = wanted_by_mate(meta_smem[0, 0])
                for part in range(2):
                    staged[1, slot, part] = own[slot][part][later_tile]
                    kv_copy(1, slot, part).start()

            def score(head):
                keys = jnp.concatenate(
                    [own[slot][0][own_tile, :, spans[head]], other[tick, slot, 0, :, spans[head]]], axis=0
                )
                return lax.dot_general(
                    queries[:, spans[head]], keys, (((1,), (1,)), ((), ())), preferred_element_type=jnp.float32
                )

            def weigh(scores):
                top = jnp.max(scores, axis=-1, keepdims=True)
                return jnp.exp2((scores - top) * to_exp2).astype(jnp.bfloat16)

            def blend(head, weights):
                values = jnp.concatenate(
                    [own[slot][1][own_tile, :, spans[head]], other[tick, slot, 1, :, spans[head]]], axis=0
                )
                return lax.dot_general(
                    weights,
                    jnp.concatenate([values, ones], axis=1),
                    (((1,), (0,)), ((), ())),
                    preferred_element_type=jnp.float32,
                )

            def settle(head, mixed):
                cols = slice(head * head_dim, (head + 1) * head_dim)
                total = mixed[:, head_dim:]
                guess = pl.reciprocal(total, approx=True)
                inverse = guess * (2.0 - total * guess)
                state[:, spans[head]] += gate[:, cols] * (mixed[:, :head_dim] * inverse)

            ahead = [score(head) for head in range(min(AHEAD, heads))]
            mixing = []
            for head in range(heads):
                if head + AHEAD < heads:
                    ahead.append(score(head + AHEAD))
                mixing.append(blend(head, weigh(ahead[head])))
                if head >= 1:
                    settle(head - 1, mixing[head - 1])
            settle(heads - 1, mixing[heads - 1])

        fin[tick, chunk] = state[...].astype(jnp.bfloat16)

        @pl.when(tick == 0)
        def _():
            state_copy(0, chunk, hold.at[1, chunk]).start()

        @pl.when(tick == 1)
        def _():
            state_copy(1, chunk, out_ref.at[chunk]).start()

        return carry

    lax.fori_loop(0, TICKS * chunks, run, 0)

    meta_copy.wait_send()
    for tick in range(TICKS):
        for slot, part in order:
            kv_copy(tick, slot, part).wait_send()
    for chunk in range(chunks):
        state_copy(0, chunk, hold.at[1, chunk]).wait_send()
        state_copy(1, chunk, out_ref.at[chunk]).wait()


def per_device(
    patches, positions, timesteps, section_bounds, tile_neighbours, modulation, query_gain, stale_kv
):
    _, tile, width = patches.shape
    _, slots, _, slab_rows, _ = stale_kv.shape
    slab_tiles = slab_rows // tile
    rows = tile // CHUNKS
    cycle = lax.axis_size("segment")
    kv = stale_kv.reshape(slots, 2, slab_tiles, tile, width)
    smem = pl.BlockSpec(memory_space=pltpu.SMEM)
    hbm = pl.BlockSpec(memory_space=pltpu.HBM)
    anywhere = pl.BlockSpec(memory_space=pl.ANY)
    dma = pltpu.SemaphoreType.DMA
    flops = TICKS * slots * 4 * tile * 2 * tile * width
    advanced = pl.pallas_call(
        functools.partial(window_kernel, cycle),
        out_shape=pltpu.VMEM((CHUNKS, rows, width), patches.dtype),
        in_specs=[smem, smem, smem, smem, hbm, hbm, hbm, hbm],
        out_specs=anywhere,
        scratch_shapes=[
            pltpu.VMEM(modulation.shape, modulation.dtype),
            pltpu.VMEM(query_gain.shape, query_gain.dtype),
            [[pltpu.VMEM(kv.shape[2:], kv.dtype) for _ in range(2)] for _ in range(slots)],
            pltpu.VMEM((TICKS, slots, 2, tile, width), kv.dtype),
            pltpu.VMEM((TICKS, slots, 2, tile, width), kv.dtype),
            pltpu.VMEM((TICKS, CHUNKS, rows, width), jnp.bfloat16),
            pltpu.VMEM((TICKS, CHUNKS, rows, width), jnp.bfloat16),
            pltpu.VMEM((rows, width), jnp.float32),
            pltpu.VMEM((rows, width), jnp.float32),
            pltpu.VMEM((width // query_gain.shape[1] * rows, query_gain.shape[1]), jnp.bfloat16),
            pltpu.VMEM((rows, width), jnp.bfloat16),
            pltpu.VMEM((8, 128), jnp.int32),
            pltpu.VMEM((8, 128), jnp.int32),
            pltpu.SMEM((8, 128), jnp.int32),
            pltpu.SMEM((TICKS, 2), jnp.int32),
            dma((slots, 2)),
            dma,
            dma,
            dma,
            dma,
            dma,
            dma,
            dma((TICKS, slots, 2)),
            dma((TICKS, slots, 2)),
            dma((TICKS, CHUNKS)),
            dma((TICKS, CHUNKS)),
        ],
        compiler_params=pltpu.CompilerParams(
            collective_id=0, has_side_effects=True, vmem_limit_bytes=58 * 2**20
        ),
        cost_estimate=pl.CostEstimate(
            flops=flops, bytes_accessed=kv.size * 2 + patches.size * 4, transcendentals=0
        ),
    )(
        positions,
        timesteps,
        section_bounds,
        tile_neighbours.T,
        modulation,
        query_gain,
        patches.reshape(CHUNKS, rows, width),
        kv,
    )
    return advanced.reshape(patches.shape)


def solution(mesh):
    placed = (
        P(("groups", "segment"), "space", None),
        P(("groups", "segment")),
        P(("groups", "segment")),
        P(),
        P(),
        P("groups", None, None, None),
        P(),
        P(("groups", "segment"), None, None, "space", None),
    )
    return jax.shard_map(
        per_device,
        mesh=mesh,
        in_specs=placed,
        out_specs=P(("groups", "segment"), "space", None),
        check_vma=False,
    )
```

```python
import functools

import jax
import jax.numpy as jnp
from jax import lax
from jax.experimental import pallas as pl
from jax.experimental.pallas import tpu as pltpu
from jax.sharding import PartitionSpec as P

TICKS = 2
CHUNKS = 2
AHEAD = 3
epsilon = 1e-06
MESH = pl.DeviceIdType.MESH


def window_kernel(
    cycle,
    pos_ref,
    step_ref,
    bounds_ref,
    near_ref,
    mod_hbm,
    gain_hbm,
    patch_ref,
    kv_ref,
    out_ref,
    mod_ref,
    gain_ref,
    own,
    staged,
    other,
    hold,
    fin,
    state,
    bent,
    squares,
    queries,
    meta_out,
    meta_in,
    meta_smem,
    table,
    own_sem,
    mod_sem,
    gain_sem,
    patch_sem,
    meta_send,
    meta_recv,
    meta_local,
    kv_send,
    kv_recv,
    state_send,
    state_recv,
):
    slots, _, slab_tiles, tile, width = kv_ref.shape
    chunks, rows = hold.shape[1], hold.shape[2]
    head_dim = gain_ref.shape[1]
    heads = width // head_dim
    pipe = bounds_ref.shape[0] - 1
    steps, layers = mod_ref.shape[0], mod_ref.shape[1]
    segment = lax.axis_index("segment")
    space = lax.axis_index("space")
    onward = lax.rem(segment + 1, cycle)
    behind = lax.rem(segment + cycle - 1, cycle)
    mate = 1 - space

    def own_copy(slot, part):
        return pltpu.make_async_copy(kv_ref.at[slot, part], own[slot][part], own_sem.at[slot, part])

    def kv_copy(tick, slot, part):
        return pltpu.make_async_remote_copy(
            src_ref=staged.at[tick, slot, part],
            dst_ref=other.at[tick, slot, part],
            send_sem=kv_send.at[tick, slot, part],
            recv_sem=kv_recv.at[tick, slot, part],
            device_id={"space": mate},
            device_id_type=MESH,
        )

    def state_copy(tick, chunk, target):
        return pltpu.make_async_remote_copy(
            src_ref=fin.at[tick, chunk],
            dst_ref=target,
            send_sem=state_send.at[tick, chunk],
            recv_sem=state_recv.at[tick, chunk],
            device_id={"segment": onward},
            device_id_type=MESH,
        )

    patch_copy = pltpu.make_async_copy(patch_ref, hold.at[0], patch_sem)
    mod_copy = pltpu.make_async_copy(mod_hbm, mod_ref, mod_sem)
    gain_copy = pltpu.make_async_copy(gain_hbm, gain_ref, gain_sem)
    meta_copy = pltpu.make_async_remote_copy(
        src_ref=meta_out,
        dst_ref=meta_in,
        send_sem=meta_send,
        recv_sem=meta_recv,
        device_id={"segment": onward},
        device_id_type=MESH,
    )
    order = [(slot, part) for slot in range(slots) for part in range(2)]
    for slot, part in order:
        own_copy(slot, part).start()
    patch_copy.start()
    mod_copy.start()
    gain_copy.start()

    barrier = pltpu.get_barrier_semaphore()
    pl.semaphore_signal(barrier, inc=1, device_id={"segment": behind}, device_id_type=MESH)
    pl.semaphore_signal(barrier, inc=1, device_id={"space": mate}, device_id_type=MESH)

    position = pos_ref[0]
    timestep = step_ref[0]
    table[0, 0] = position
    table[0, 1] = timestep
    lane = lax.broadcasted_iota(jnp.int32, meta_out.shape, 1)
    meta_out[...] = jnp.where(lane == 0, position, timestep)
    pl.semaphore_wait(barrier, 2)
    meta_copy.start()

    def wanted_by_mate(pos):
        return lax.rem(near_ref[1, mate * slab_tiles + pos], slab_tiles)

    mate_tile = wanted_by_mate(position)

    def send_first(slot):
        for part in range(2):
            own_copy(slot, part).wait()
            staged[0, slot, part] = own[slot][part][mate_tile]
            kv_copy(0, slot, part).start()

    send_first(0)
    patch_copy.wait()
    mod_copy.wait()
    gain_copy.wait()

    section = lax.rem(segment, pipe)
    first_layer = bounds_ref[section]
    layer_count = bounds_ref[section + 1] - first_layer
    to_exp2 = head_dim ** (-0.5) * 1.4426950408889634

    ones = jnp.ones((2 * tile, head_dim), jnp.bfloat16)

    def run(index, carry):
        tick = index // chunks
        chunk = lax.rem(index, chunks)

        @pl.when(index == 1)
        def _():
            meta_copy.wait_recv()
            to_smem = pltpu.make_async_copy(meta_in, meta_smem, meta_local)
            to_smem.start()
            to_smem.wait()
            table[1, 0] = meta_smem[0, 0]
            table[1, 1] = meta_smem[0, 1]
            later_tile = wanted_by_mate(meta_smem[0, 0])
            for slot, part in order:
                staged[1, slot, part] = own[slot][part][later_tile]
                kv_copy(1, slot, part).start()

        @pl.when(tick == 1)
        def _():
            state_copy(0, chunk, hold.at[1, chunk]).wait_recv()

        root = lax.rem(segment - tick + cycle, cycle)
        crossed = jnp.where(lax.rem(root, pipe) + tick >= pipe, 1, 0)
        step_row = jnp.minimum(table[tick, 1] + crossed, steps - 1)
        own_tile = lax.rem(near_ref[0, space * slab_tiles + table[tick, 0]], slab_tiles)
        state[...] = hold[tick, chunk].astype(jnp.float32)

        for slot in range(slots):
            layer = jnp.minimum(first_layer + slot, layers - 1)
            mod = mod_ref[step_row, layer].astype(jnp.float32)
            gain = gain_ref[pl.ds(layer, 1), :]
            active = jnp.where(slot < layer_count, 1.0, 0.0)
            gate = mod[2:3] * active
            spans = [pl.ds(head * head_dim, head_dim) for head in range(heads)]
            total = state[:, spans[0]]
            for span in spans[1:]:
                total = total + state[:, span]
            middle = jnp.sum(total, axis=-1, keepdims=True) * (1.0 / width)
            total = jnp.zeros((rows, head_dim), jnp.float32)
            for span in spans:
                centred = state[:, span] - middle
                total = total + centred * centred
            spread = jnp.sum(total, axis=-1, keepdims=True) * (1.0 / width)
            scale = lax.rsqrt(spread + epsilon)
            for head, span in enumerate(spans):
                cols = slice(head * head_dim, (head + 1) * head_dim)
                normed = (state[:, span] - middle) * scale
                shifted = normed * (1.0 + mod[1:2, cols]) + mod[0:1, cols]
                bent[:, span] = shifted
                squares[pl.ds(head * rows, rows), :] = (shifted * shifted).astype(jnp.bfloat16)
            square_sums = jnp.dot(squares[...], ones[:head_dim], preferred_element_type=jnp.float32)
            for head, span in enumerate(spans):
                rms = square_sums[head * rows : (head + 1) * rows] * (1.0 / head_dim)
                queries[:, span] = (bent[:, span] * lax.rsqrt(rms + epsilon) * gain).astype(jnp.bfloat16)

            if slot + 1 < slots:
                pl.when(index == 0)(functools.partial(send_first, slot + 1))

            @pl.when(chunk == 0)
            def _():
                for part in range(2):
                    kv_copy(tick, slot, part).wait_recv()

            def score(head):
                keys = jnp.concatenate(
                    [own[slot][0][own_tile, :, spans[head]], other[tick, slot, 0, :, spans[head]]], axis=0
                )
                return lax.dot_general(
                    queries[:, spans[head]], keys, (((1,), (1,)), ((), ())), preferred_element_type=jnp.float32
                )

            def weigh(scores):
                top = jnp.max(scores, axis=-1, keepdims=True)
                return jnp.exp2((scores - top) * to_exp2).astype(jnp.bfloat16)

            def blend(head, weights):
                values = jnp.concatenate(
                    [own[slot][1][own_tile, :, spans[head]], other[tick, slot, 1, :, spans[head]]], axis=0
                )
                return lax.dot_general(
                    weights,
                    jnp.concatenate([values, ones], axis=1),
                    (((1,), (0,)), ((), ())),
                    preferred_element_type=jnp.float32,
                )

            def settle(head, mixed):
                cols = slice(head * head_dim, (head + 1) * head_dim)
                total = mixed[:, head_dim:]
                guess = pl.reciprocal(total, approx=True)
                inverse = guess * (2.0 - total * guess)
                state[:, spans[head]] += gate[:, cols] * (mixed[:, :head_dim] * inverse)

            ahead = [score(head) for head in range(min(AHEAD, heads))]
            mixing = []
            for head in range(heads):
                if head + AHEAD < heads:
                    ahead.append(score(head + AHEAD))
                mixing.append(blend(head, weigh(ahead[head])))
                if head >= 1:
                    settle(head - 1, mixing[head - 1])
            settle(heads - 1, mixing[heads - 1])

        fin[tick, chunk] = state[...].astype(jnp.bfloat16)

        @pl.when(tick == 0)
        def _():
            state_copy(0, chunk, hold.at[1, chunk]).start()

        @pl.when(tick == 1)
        def _():
            state_copy(1, chunk, out_ref.at[chunk]).start()

        return carry

    lax.fori_loop(0, TICKS * chunks, run, 0)

    meta_copy.wait_send()
    for tick in range(TICKS):
        for slot, part in order:
            kv_copy(tick, slot, part).wait_send()
    for chunk in range(chunks):
        state_copy(0, chunk, hold.at[1, chunk]).wait_send()
        state_copy(1, chunk, out_ref.at[chunk]).wait()


def per_device(
    patches, positions, timesteps, section_bounds, tile_neighbours, modulation, query_gain, stale_kv
):
    _, tile, width = patches.shape
    _, slots, _, slab_rows, _ = stale_kv.shape
    slab_tiles = slab_rows // tile
    rows = tile // CHUNKS
    cycle = lax.axis_size("segment")
    kv = stale_kv.reshape(slots, 2, slab_tiles, tile, width)
    smem = pl.BlockSpec(memory_space=pltpu.SMEM)
    hbm = pl.BlockSpec(memory_space=pltpu.HBM)
    anywhere = pl.BlockSpec(memory_space=pl.ANY)
    dma = pltpu.SemaphoreType.DMA
    flops = TICKS * slots * 4 * tile * 2 * tile * width
    advanced = pl.pallas_call(
        functools.partial(window_kernel, cycle),
        out_shape=pltpu.VMEM((CHUNKS, rows, width), patches.dtype),
        in_specs=[smem, smem, smem, smem, hbm, hbm, hbm, hbm],
        out_specs=anywhere,
        scratch_shapes=[
            pltpu.VMEM(modulation.shape, modulation.dtype),
            pltpu.VMEM(query_gain.shape, query_gain.dtype),
            [[pltpu.VMEM(kv.shape[2:], kv.dtype) for _ in range(2)] for _ in range(slots)],
            pltpu.VMEM((TICKS, slots, 2, tile, width), kv.dtype),
            pltpu.VMEM((TICKS, slots, 2, tile, width), kv.dtype),
            pltpu.VMEM((TICKS, CHUNKS, rows, width), jnp.bfloat16),
            pltpu.VMEM((TICKS, CHUNKS, rows, width), jnp.bfloat16),
            pltpu.VMEM((rows, width), jnp.float32),
            pltpu.VMEM((rows, width), jnp.float32),
            pltpu.VMEM((width // query_gain.shape[1] * rows, query_gain.shape[1]), jnp.bfloat16),
            pltpu.VMEM((rows, width), jnp.bfloat16),
            pltpu.VMEM((8, 128), jnp.int32),
            pltpu.VMEM((8, 128), jnp.int32),
            pltpu.SMEM((8, 128), jnp.int32),
            pltpu.SMEM((TICKS, 2), jnp.int32),
            dma((slots, 2)),
            dma,
            dma,
            dma,
            dma,
            dma,
            dma,
            dma((TICKS, slots, 2)),
            dma((TICKS, slots, 2)),
            dma((TICKS, CHUNKS)),
            dma((TICKS, CHUNKS)),
        ],
        compiler_params=pltpu.CompilerParams(
            collective_id=0, has_side_effects=True, vmem_limit_bytes=58 * 2**20
        ),
        cost_estimate=pl.CostEstimate(
            flops=flops, bytes_accessed=kv.size * 2 + patches.size * 4, transcendentals=0
        ),
    )(
        positions,
        timesteps,
        section_bounds,
        tile_neighbours.T,
        modulation,
        query_gain,
        patches.reshape(CHUNKS, rows, width),
        kv,
    )
    return advanced.reshape(patches.shape)


def solution(mesh):
    placed = (
        P(("groups", "segment"), "space", None),
        P(("groups", "segment")),
        P(("groups", "segment")),
        P(),
        P(),
        P("groups", None, None, None),
        P(),
        P(("groups", "segment"), None, None, "space", None),
    )
    return jax.shard_map(
        per_device,
        mesh=mesh,
        in_specs=placed,
        out_specs=P(("groups", "segment"), "space", None),
        check_vma=False,
    )
```
